128 devices in a mesh: hi: 16 (over z, x), lo: 8 (over y, core).
Axes of the slice: x: 4, y: 4, z: 4, core: 2. Of those that a mesh axis runs over, the one named last changes fastest.
Arguments:
- sources: bfloat16 [64, 2097152], P(None, ('hi', 'lo')), may hold values from -6 to 6
- leaf_in: bfloat16 [8192, 64, 256], P(('hi', 'lo')), may hold values from -0.375 to 0.375
- local_mix: bfloat16 [8192, 6, 64, 128], P(('hi', 'lo')), may hold values from -0.5 to 0.5
- lo_mix: bfloat16 [8192, 3, 64, 128], P(('hi', 'lo')), may hold values from -0.5 to 0.5
- hi_mix: bfloat16 [8192, 4, 64, 128], P(('hi', 'lo')), may hold values from -0.5 to 0.5
- leaf_out: bfloat16 [8192, 64, 256], P(('hi', 'lo')), may hold values from -0.75 to 0.75
Outputs:
- targets: bfloat16 [64, 2097152], P(None, ('hi', 'lo'))
The draws below stay inside these ranges and needn't reach their ends.
All inputs are finite; a program needn't handle non-finite values.
Results may differ from the reference program's by a relative error of at most 0.029.
Values may be sent and summed in bfloat16 or wider, within the bound.
A program may use at most 128 MiB of HBM per device.

```python
import jax
import jax.numpy as jnp

RANK = 64
LEAF = 256
VECS = 64
LOC_LEV = 6
LO_BITS = 3
HI_BITS = 4
BLOCKS = 8192
POINTS = 2097152


def level_of(stream_key, shape, cuts, low, largest):
    def one(position, blocks):
        draws = jax.random.uniform(jax.random.fold_in(jax.random.fold_in(stream_key, 6), position), (blocks,), jnp.float32, low / len(cuts), largest / len(cuts))
        return jnp.repeat(jnp.exp(draws), shape[position] // blocks).reshape((-1,) + (1,) * (len(shape) - position - 1))

    loudness = one(*cuts[0])
    for cut in cuts[1:]:
        loudness = loudness * one(*cut)
    return loudness


def gaussian(key, dims, scale, limit, split=(), kind=jnp.bfloat16):
    array = jax.random.normal(key, dims, jnp.float32) * scale
    if len(split) > 0:
        array = level_of(key, dims, split, -0.22, 0.18) * array
    return jnp.clip(array, min=-limit, max=limit).astype(kind)


def setup_inputs(seed: int = 0) -> dict:
    seeds = jax.random.split(jax.random.key(seed), 7)
    return {
        "sources": gaussian(seeds[0], (VECS, POINTS), 1.0, 6.0, ((1, 128),)),
        "leaf_in": gaussian(seeds[1], (BLOCKS, RANK, LEAF), LEAF ** -0.5, 0.375, ((0, 128),)),
        "local_mix": gaussian(seeds[2], (BLOCKS, LOC_LEV, RANK, 2 * RANK), (2 * RANK) ** -0.5, 0.5, ((0, 128),)),
        "lo_mix": gaussian(seeds[3], (BLOCKS, LO_BITS, RANK, 2 * RANK), (2 * RANK) ** -0.5, 0.5, ((0, 128),)),
        "hi_mix": gaussian(seeds[4], (BLOCKS, HI_BITS, RANK, 2 * RANK), (2 * RANK) ** -0.5, 0.5, ((0, 128),)),
        "leaf_out": gaussian(seeds[5], (BLOCKS, RANK, LEAF), RANK ** -0.5, 0.75, ((0, 128),)),
    }


def flip_blocks(current, level_bit):
    shape_now = current.shape
    grouped = current.reshape((shape_now[0] >> (level_bit + 1), 2, 1 << level_bit) + shape_now[1:])
    return grouped[:, ::-1].reshape(shape_now)


def mix_level(current, partner, factors):
    joined = jnp.concatenate([current, partner], axis=-1).astype(jnp.float32)
    mixed = jnp.einsum("kvs,kqs->kvq", joined, factors.astype(jnp.float32))
    return mixed.astype(jnp.bfloat16)


def reference(sources, leaf_in, local_mix, lo_mix, hi_mix, leaf_out):
    blocks_all = leaf_in.shape[0]
    leaf_size = leaf_in.shape[2]
    vectors = sources.shape[0]
    source_blocks = sources.reshape(vectors, blocks_all, leaf_size).astype(jnp.float32)
    current = jnp.einsum("vkl,krl->kvr", source_blocks, leaf_in.astype(jnp.float32)).astype(jnp.bfloat16)
    level_bit = 0
    for level in range(LOC_LEV):
        current = mix_level(current, flip_blocks(current, level_bit), local_mix[:, level])
        level_bit = level_bit + 1
    for level in range(LO_BITS):
        current = mix_level(current, flip_blocks(current, level_bit), lo_mix[:, level])
        level_bit = level_bit + 1
    for level in range(HI_BITS):
        current = mix_level(current, flip_blocks(current, level_bit), hi_mix[:, level])
        level_bit = level_bit + 1
    result = jnp.einsum("kvr,krl->vkl", current.astype(jnp.float32), leaf_out.astype(jnp.float32))
    return result.reshape(vectors, blocks_all * leaf_size).astype(jnp.bfloat16)
```

```python
import functools

import jax
import jax.numpy as jnp
from jax import lax
from jax.experimental import pallas as pl
from jax.experimental.pallas import tpu as pltpu
from jax.sharding import PartitionSpec as P

MESH = pl.DeviceIdType.MESH
GROUP = 1
OFFSETS = (0, 2, 5, 8, 11, 14, 17, 20)
CHUNKS = 4
UNROLL = 4


def low_lanes(shape):
    return lax.broadcasted_iota(jnp.int32, shape, len(shape) - 1) < shape[-1] // 2


def mixed(own, partner, f_low, f_high):
    zero = jnp.zeros_like(own)
    low = low_lanes(own.shape)
    rhs = jnp.concatenate(
        [
            jnp.where(low, own, zero),
            jnp.where(low, partner, zero),
            jnp.where(low, zero, own),
            jnp.where(low, zero, partner),
        ],
        axis=0,
    )
    lhs = jnp.concatenate([f_low, f_high], axis=1)
    return jnp.dot(lhs, rhs, preferred_element_type=jnp.float32).astype(jnp.bfloat16)


def kernel(
    lo_levels,
    hi_levels,
    sources,
    leaf_in,
    local_mix,
    lo_mix,
    hi_mix,
    leaf_out,
    targets,
    src_v,
    in_v,
    loc_v,
    mix_v,
    out_v,
    tgt_v,
    work,
    own,
    recv,
    in_sem,
    loc_sem,
    mix_sem,
    out_sem,
    tgt_sem,
    send_sem,
    recv_sem,
):
    blocks, rank, leaf = leaf_in.shape
    vecs = sources.shape[0]
    half = blocks // 2
    local_levels = local_mix.shape[1]
    levels = lo_levels + hi_levels
    groups = half // GROUP
    hi, lo = lax.axis_index("hi"), lax.axis_index("lo")

    def flipped(index, bit):
        stride = 1 << bit
        return index + stride - 2 * stride * ((index // stride) % 2)

    partners = [(hi, flipped(lo, b)) for b in range(lo_levels)]
    partners += [(flipped(hi, b), lo) for b in range(hi_levels)]

    barrier = pltpu.get_barrier_semaphore()
    for partner in partners:
        pl.semaphore_signal(barrier, inc=1, device_id=partner, device_id_type=MESH)

    part = half // CHUNKS
    in_copies = []
    for c in range(CHUNKS):
        copies = []
        for side in range(2):
            first = side * half + c * part
            columns = pl.ds(first * leaf, part * leaf)
            rows = pl.ds(first, part)
            copies.append(
                pltpu.make_async_copy(
                    sources.at[:, columns], src_v.at[:, columns], in_sem.at[c, 2 * side]
                )
            )
            copies.append(
                pltpu.make_async_copy(leaf_in.at[rows], in_v.at[rows], in_sem.at[c, 2 * side + 1])
            )
        in_copies.append(copies)
    loc_copies = [
        pltpu.make_async_copy(local_mix.at[:, b], loc_v.at[b], loc_sem.at[b])
        for b in range(local_levels)
    ]
    mix_copies = [
        pltpu.make_async_copy(lo_mix.at[:, b], mix_v.at[b], mix_sem.at[b]) for b in range(lo_levels)
    ]
    mix_copies += [
        pltpu.make_async_copy(hi_mix.at[:, b], mix_v.at[lo_levels + b], mix_sem.at[lo_levels + b])
        for b in range(hi_levels)
    ]
    out_copy = pltpu.make_async_copy(leaf_out, out_v, out_sem.at[0])
    for copies in in_copies:
        for copy in copies:
            copy.start()
    for copy in loc_copies + mix_copies + [out_copy]:
        copy.start()

    for c in range(CHUNKS):
        for copy in in_copies[c]:
            copy.wait()

        def project(i, _):
            for u in range(UNROLL):
                j = c * part + i * UNROLL + u
                lhs = jnp.concatenate([in_v[j], in_v[j + half]], axis=0)
                low = pl.ds(pl.multiple_of(j * leaf, leaf), leaf)
                high = pl.ds(pl.multiple_of((j + half) * leaf, leaf), leaf)
                rhs = jnp.concatenate([src_v[:, low], src_v[:, high]], axis=0)
                both = lax.dot_general(
                    lhs, rhs, (((1,), (1,)), ((), ())), preferred_element_type=jnp.float32
                )
                tile = jnp.where(low_lanes((rank, 2 * vecs)), both[:rank], both[rank:])
                work[0, j] = tile.astype(jnp.bfloat16)
            return 0

        lax.fori_loop(0, part // UNROLL, project, 0)

    for b in range(local_levels - 1):
        loc_copies[b].wait()
        stride = 1 << b
        now, later = b % 2, (b + 1) % 2

        def pair(i, _):
            for u in range(UNROLL // 2):
                p = i * (UNROLL // 2) + u
                j = (p // stride) * (2 * stride) + p % stride
                k = j + stride
                first, second = work[now, j], work[now, k]
                work[later, j] = mixed(first, second, loc_v[b, j], loc_v[b, j + half])
                work[later, k] = mixed(second, first, loc_v[b, k], loc_v[b, k + half])
            return 0

        lax.fori_loop(0, half // UNROLL, pair, 0)
    final = (local_levels - 1) % 2
    loc_copies[local_levels - 1].wait()
    pl.semaphore_wait(barrier, levels)
    for copy in mix_copies + [out_copy]:
        copy.wait()

    def message(stage, g):
        tiles = pl.ds(g * GROUP, GROUP)
        return pltpu.make_async_remote_copy(
            own.at[stage, tiles],
            recv.at[stage, tiles],
            send_sem.at[stage],
            recv_sem.at[stage, g],
            device_id=partners[stage],
            device_id_type=MESH,
        )

    def run_stage(stage, g):
        if stage > 0:
            message(stage - 1, g).wait_recv()
        for u in range(GROUP):
            j = g * GROUP + u
            if stage == 0:
                tile = work[final, j]
                turned = jnp.concatenate([tile[:, vecs:], tile[:, :vecs]], axis=1)
                b = local_levels - 1
                own[0, j] = mixed(tile, turned, loc_v[b, j], loc_v[b, j + half])
            else:
                tile = mixed(
                    own[stage - 1, j],
                    recv[stage - 1, j],
                    mix_v[stage - 1, j],
                    mix_v[stage - 1, j + half],
                )
                if stage < levels:
                    own[stage, j] = tile
                else:
                    flat = tile.T
                    for side in range(2):
                        block = j + side * half
                        columns = pl.ds(pl.multiple_of(block * leaf, leaf), leaf)
                        result = jnp.dot(
                            flat[side * vecs : (side + 1) * vecs],
                            out_v[block],
                            preferred_element_type=jnp.float32,
                        )
                        tgt_v[:, columns] = result.astype(jnp.bfloat16)
        if stage < levels:
            message(stage, g).start()
        else:
            for side in range(2):
                start = (side * half + g * GROUP) * leaf
                columns = pl.ds(pl.multiple_of(start, leaf), GROUP * leaf)
                pltpu.make_async_copy(
                    tgt_v.at[:, columns], targets.at[:, columns], tgt_sem.at[0]
                ).start()

    def step(t, _):
        for stage in reversed(range(levels + 1)):
            g = t - OFFSETS[stage]

            @pl.when((g >= 0) & (g < groups))
            def _():
                run_stage(stage, g)

        return 0

    lax.fori_loop(0, groups + OFFSETS[levels], step, 0)

    for stage in range(levels):
        pltpu.make_async_remote_copy(
            own.at[stage],
            recv.at[stage],
            send_sem.at[stage],
            recv_sem.at[stage, 0],
            device_id=partners[stage],
            device_id_type=MESH,
        ).wait_send()
    pltpu.make_async_copy(tgt_v, targets, tgt_sem.at[0]).wait()


def body(sources, leaf_in, local_mix, lo_mix, hi_mix, leaf_out):
    blocks, rank, leaf = leaf_in.shape
    vecs = sources.shape[0]
    local_levels = local_mix.shape[1]
    lo_levels, hi_levels = lo_mix.shape[1], hi_mix.shape[1]
    levels = lo_levels + hi_levels
    half = blocks // 2
    tiles = (half, rank, 2 * vecs)
    dma = pltpu.SemaphoreType.DMA
    return pl.pallas_call(
        functools.partial(kernel, lo_levels, hi_levels),
        out_shape=jax.ShapeDtypeStruct(sources.shape, jnp.bfloat16),
        in_specs=[pl.BlockSpec(memory_space=pl.ANY)] * 6,
        out_specs=pl.BlockSpec(memory_space=pl.ANY),
        scratch_shapes=[
            pltpu.VMEM(sources.shape, jnp.bfloat16),
            pltpu.VMEM(leaf_in.shape, jnp.bfloat16),
            pltpu.VMEM((local_levels, blocks) + local_mix.shape[2:], jnp.bfloat16),
            pltpu.VMEM((levels, blocks) + local_mix.shape[2:], jnp.bfloat16),
            pltpu.VMEM(leaf_out.shape, jnp.bfloat16),
            pltpu.VMEM(sources.shape, jnp.bfloat16),
            pltpu.VMEM((2,) + tiles, jnp.bfloat16),
            pltpu.VMEM((levels,) + tiles, jnp.bfloat16),
            pltpu.VMEM((levels,) + tiles, jnp.bfloat16),
            dma((CHUNKS, 4)),
            dma((local_levels,)),
            dma((levels,)),
            dma((1,)),
            dma((1,)),
            dma((levels,)),
            dma((levels, half // GROUP)),
        ],
        compiler_params=pltpu.CompilerParams(
            collective_id=0, has_side_effects=True, vmem_limit_bytes=48 * 1024 * 1024
        ),
        name="butterfly",
    )(sources, leaf_in, local_mix, lo_mix, hi_mix, leaf_out)


def solution(mesh):
    return jax.shard_map(
        body,
        mesh=mesh,
        in_specs=(
            P(None, ("hi", "lo")),
            P(("hi", "lo"), None, None),
            P(("hi", "lo"), None, None, None),
            P(("hi", "lo"), None, None, None),
            P(("hi", "lo"), None, None, None),
            P(("hi", "lo"), None, None),
        ),
        out_specs=P(None, ("hi", "lo")),
        check_vma=False,
    )
```

```python
import functools

import jax
import jax.numpy as jnp
from jax import lax
from jax.experimental import pallas as pl
from jax.experimental.pallas import tpu as pltpu
from jax.sharding import PartitionSpec as P

MESH = pl.DeviceIdType.MESH
GROUP = 1
DELAYS = (2, 4, 5, 4, 5, 4, 5)
CHUNKS = 4
UNROLL = 16


def low_lanes(shape):
    return lax.broadcasted_iota(jnp.int32, shape, len(shape) - 1) < shape[-1] // 2


def mixed(own, partner, f_low, f_high):
    zero = jnp.zeros_like(own)
    low = low_lanes(own.shape)
    rhs = jnp.concatenate(
        [
            jnp.where(low, own, zero),
            jnp.where(low, partner, zero),
            jnp.where(low, zero, own),
            jnp.where(low, zero, partner),
        ],
        axis=0,
    )
    lhs = jnp.concatenate([f_low, f_high], axis=1)
    return jnp.dot(lhs, rhs, preferred_element_type=jnp.float32).astype(jnp.bfloat16)


def kernel(lo_levels, hi_levels, *refs):
    levels = lo_levels + hi_levels
    sources, leaf_in, local_mix, lo_mix, hi_mix, leaf_out, targets = refs[:7]
    src_v, in_v, loc_v, mix_v, out_v = refs[7:12]
    work = refs[12:14]
    own = refs[14 : 15 + levels]
    recv = refs[15 + levels : 15 + 2 * levels]
    in_sem, loc_sem, mix_sem, out_sem, send_sem, recv_sem = refs[15 + 2 * levels :]
    blocks, rank, leaf = leaf_in.shape
    vecs = sources.shape[0]
    half = blocks // 2
    local_levels = local_mix.shape[1]
    groups = half // GROUP
    hi, lo = lax.axis_index("hi"), lax.axis_index("lo")

    def flipped(index, bit):
        stride = 1 << bit
        return index + stride - 2 * stride * ((index // stride) % 2)

    partners = [(hi, flipped(lo, b)) for b in range(lo_levels)]
    partners += [(flipped(hi, b), lo) for b in range(hi_levels)]

    barrier = pltpu.get_barrier_semaphore()
    for partner in partners:
        pl.semaphore_signal(barrier, inc=1, device_id=partner, device_id_type=MESH)

    part = half // CHUNKS
    in_copies = []
    for c in range(CHUNKS):
        copies = []
        for side in range(2):
            first = side * half + c * part
            columns = pl.ds(first * leaf, part * leaf)
            rows = pl.ds(first, part)
            copies.append(
                pltpu.make_async_copy(
                    sources.at[:, columns], src_v.at[:, columns], in_sem.at[c, 2 * side]
                )
            )
            copies.append(
                pltpu.make_async_copy(leaf_in.at[rows], in_v.at[rows], in_sem.at[c, 2 * side + 1])
            )
        in_copies.append(copies)
    loc_copies = [
        pltpu.make_async_copy(local_mix.at[:, b], loc_v.at[b], loc_sem.at[b])
        for b in range(local_levels)
    ]
    held = pl.ds(GROUP, half)
    mix_copies, out_copies = [], []
    for b in range(levels):
        mix = lo_mix.at[:, b] if b < lo_levels else hi_mix.at[:, b - lo_levels]
        mix_copies.append(
            [
                pltpu.make_async_copy(
                    mix.at[pl.ds(side * half, half)], mix_v.at[b, side, held], mix_sem.at[b, side]
                )
                for side in range(2)
            ]
        )
    for side in range(2):
        out_copies.append(
            pltpu.make_async_copy(
                leaf_out.at[pl.ds(side * half, half)], out_v.at[side, held], out_sem.at[side]
            )
        )
    for copies in in_copies + [loc_copies] + mix_copies + [out_copies]:
        for copy in copies:
            copy.start()

    for c in range(CHUNKS):
        for copy in in_copies[c]:
            copy.wait()
        for j in range(c * part, (c + 1) * part):
            lhs = jnp.concatenate([in_v[j], in_v[j + half]], axis=0)
            low, high = pl.ds(j * leaf, leaf), pl.ds((j + half) * leaf, leaf)
            rhs = jnp.concatenate([src_v[:, low], src_v[:, high]], axis=0)
            both = lax.dot_general(
                lhs, rhs, (((1,), (1,)), ((), ())), preferred_element_type=jnp.float32
            )
            tile = jnp.where(low_lanes((rank, 2 * vecs)), both[:rank], both[rank:])
            work[0][j] = tile.astype(jnp.bfloat16)

    for b in range(local_levels - 1):
        loc_copies[b].wait()
        stride = 1 << b
        now, later = work[b % 2], work[(b + 1) % 2]

        def pair(i, _):
            for u in range(UNROLL // 2):
                p = i * (UNROLL // 2) + u
                j = (p // stride) * (2 * stride) + p % stride
                k = j + stride
                first, second = now[j], now[k]
                later[j] = mixed(first, second, loc_v[b, j], loc_v[b, j + half])
                later[k] = mixed(second, first, loc_v[b, k], loc_v[b, k + half])
            return 0

        lax.fori_loop(0, half // UNROLL, pair, 0)
    last = local_levels - 1
    entered = work[last % 2]
    loc_copies[last].wait()
    pl.semaphore_wait(barrier, levels)

    starts = [0]
    for delay in DELAYS[:levels]:
        starts.append(starts[-1] + delay)
    starts.append(starts[-1] + 1)

    def message(stage, g):
        tiles = pl.ds((g + 1) * GROUP, GROUP)
        return pltpu.make_async_remote_copy(
            own[stage].at[tiles],
            recv[stage].at[tiles],
            send_sem.at[stage],
            recv_sem.at[stage, g],
            device_id=partners[stage],
            device_id_type=MESH,
        )

    def step(t, _):
        for stage in range(levels + 1):
            g = t - starts[stage]
            if stage > 0:

                @pl.when((g >= 0) & (g < groups))
                def _():
                    message(stage - 1, g).wait_recv()

                @pl.when(g == 0)
                def _():
                    for copy in mix_copies[stage - 1]:
                        copy.wait()

        @pl.when(t == starts[levels + 1])
        def _():
            for copy in out_copies:
                copy.wait()

        for u in range(GROUP):
            g = t - starts[levels + 1]
            place = (jnp.maximum(g, -1) + 1) * GROUP + u
            j = jnp.maximum(g, 0) * GROUP + u
            flat = own[levels][place].T
            for side in range(2):
                block = j + side * half
                columns = pl.ds(pl.multiple_of(block * leaf, leaf), leaf)
                result = jnp.dot(
                    flat[side * vecs : (side + 1) * vecs],
                    out_v[side, place],
                    preferred_element_type=jnp.float32,
                )
                targets[:, columns] = result.astype(jnp.bfloat16)
            for stage in reversed(range(levels + 1)):
                g = t - starts[stage]
                place = (jnp.minimum(jnp.maximum(g, -1), groups) + 1) * GROUP + u
                known = jnp.minimum(place, half + u)
                j = jnp.minimum(jnp.maximum(g, 0), groups - 1) * GROUP + u
                if stage > 0:
                    own[stage][place] = mixed(
                        own[stage - 1][place],
                        recv[stage - 1][place],
                        mix_v[stage - 1, 0, known],
                        mix_v[stage - 1, 1, known],
                    )
                else:
                    tile = entered[j]
                    turned = jnp.concatenate([tile[:, vecs:], tile[:, :vecs]], axis=1)
                    own[0][place] = mixed(tile, turned, loc_v[last, j], loc_v[last, j + half])

        for stage in range(levels):
            g = t - starts[stage]

            @pl.when((g >= 0) & (g < groups))
            def _():
                message(stage, g).start()

        return 0

    lax.fori_loop(0, groups + starts[levels + 1], step, 0)

    for stage in range(levels):
        pltpu.make_async_remote_copy(
            own[stage].at[held],
            recv[stage].at[held],
            send_sem.at[stage],
            recv_sem.at[stage, 0],
            device_id=partners[stage],
            device_id_type=MESH,
        ).wait_send()


def body(sources, leaf_in, local_mix, lo_mix, hi_mix, leaf_out):
    blocks, rank, _ = leaf_in.shape
    vecs = sources.shape[0]
    local_levels = local_mix.shape[1]
    lo_levels, hi_levels = lo_mix.shape[1], hi_mix.shape[1]
    levels = lo_levels + hi_levels
    half = blocks // 2
    factors = (blocks,) + local_mix.shape[2:]
    bf16, dma = jnp.bfloat16, pltpu.SemaphoreType.DMA
    spared = pltpu.VMEM((half + 2 * GROUP, rank, 2 * vecs), bf16)
    return pl.pallas_call(
        functools.partial(kernel, lo_levels, hi_levels),
        out_shape=jax.ShapeDtypeStruct(sources.shape, bf16),
        in_specs=[pl.BlockSpec(memory_space=pltpu.HBM)] * 6,
        out_specs=pl.BlockSpec(memory_space=pltpu.VMEM),
        scratch_shapes=[
            pltpu.VMEM(sources.shape, bf16),
            pltpu.VMEM(leaf_in.shape, bf16),
            pltpu.VMEM((local_levels,) + factors, bf16),
            pltpu.VMEM((levels, 2, half + GROUP) + factors[1:], bf16),
            pltpu.VMEM((2, half + GROUP) + leaf_out.shape[1:], bf16),
        ]
        + [pltpu.VMEM((half, rank, 2 * vecs), bf16)] * 2
        + [spared] * (2 * levels + 1)
        + [
            dma((CHUNKS, 4)),
            dma((local_levels,)),
            dma((levels, 2)),
            dma((2,)),
            dma((levels,)),
            dma((levels, half // GROUP)),
        ],
        compiler_params=pltpu.CompilerParams(
            collective_id=0, has_side_effects=True, vmem_limit_bytes=50 * 1024 * 1024
        ),
        name="butterfly",
    )(sources, leaf_in, local_mix, lo_mix, hi_mix, leaf_out)


def solution(mesh):
    return jax.shard_map(
        body,
        mesh=mesh,
        in_specs=(
            P(None, ("hi", "lo")),
            P(("hi", "lo"), None, None),
            P(("hi", "lo"), None, None, None),
            P(("hi", "lo"), None, None, None),
            P(("hi", "lo"), None, None, None),
            P(("hi", "lo"), None, None),
        ),
        out_specs=P(None, ("hi", "lo")),
        check_vma=False,
    )
```

```python
import functools

import jax
import jax.numpy as jnp
from jax import lax
from jax.experimental import pallas as pl
from jax.experimental.pallas import tpu as pltpu
from jax.sharding import PartitionSpec as P

MESH = pl.DeviceIdType.MESH
EARLY = 1
LOCAT = 1
LATE = 1
GROUP = 1
DELAYS = (2, 5, 6, 5, 6, 5, 6)
CHUNKS = 4
BLOCKS = ((8, 7, 6, 5), (4, 3, 2, 1, 0))
UNROLL = 32


def low_lanes(shape):
    return lax.broadcasted_iota(jnp.int32, shape, len(shape) - 1) < shape[-1] // 2


def mixed(own, partner, f_low, f_high):
    zero = jnp.zeros_like(own)
    low = low_lanes(own.shape)
    rhs = jnp.concatenate(
        [
            jnp.where(low, own, zero),
            jnp.where(low, partner, zero),
            jnp.where(low, zero, own),
            jnp.where(low, zero, partner),
        ],
        axis=0,
    )
    lhs = jnp.concatenate([f_low, f_high], axis=1)
    return jnp.dot(lhs, rhs, preferred_element_type=jnp.float32).astype(jnp.bfloat16)


def kernel(lo_levels, hi_levels, *refs):
    levels = lo_levels + hi_levels
    sources, leaf_in, local_mix, lo_mix, hi_mix, leaf_out, targets = refs[:7]
    src_v, in_v, loc_v, mix_v, out_v = refs[7:12]
    work = refs[12:14]
    own = refs[14 : 15 + levels]
    recv = refs[15 + levels : 15 + 2 * levels]
    in_sem, loc_sem, mix_sem, out_sem, send_sem, recv_sem = refs[15 + 2 * levels :]
    blocks, rank, leaf = leaf_in.shape
    vecs = sources.shape[0]
    half = blocks // 2
    local_levels = local_mix.shape[1]
    groups = half // GROUP
    hi, lo = lax.axis_index("hi"), lax.axis_index("lo")

    def flipped(index, bit):
        stride = 1 << bit
        return index + stride - 2 * stride * ((index // stride) % 2)

    partners = [(hi, flipped(lo, b)) for b in range(lo_levels)]
    partners += [(flipped(hi, b), lo) for b in range(hi_levels)]

    barrier = pltpu.get_barrier_semaphore()
    for partner in partners:
        pl.semaphore_signal(barrier, inc=1, device_id=partner, device_id_type=MESH)

    part = half // CHUNKS
    in_copies = []
    for c in range(CHUNKS):
        copies = []
        for side in range(2):
            first = side * half + c * part
            columns = pl.ds(first * leaf, part * leaf)
            rows = pl.ds(first, part)
            copies.append(
                pltpu.make_async_copy(
                    sources.at[:, columns], src_v.at[:, columns], in_sem.at[c, 2 * side]
                )
            )
            copies.append(
                pltpu.make_async_copy(leaf_in.at[rows], in_v.at[rows], in_sem.at[c, 2 * side + 1])
            )
        in_copies.append(copies)
    loc_copies = [
        pltpu.make_async_copy(local_mix.at[:, b], loc_v.at[b], loc_sem.at[b])
        for b in range(local_levels)
    ]
    held = pl.ds(GROUP, half)
    mix_copies, out_copies = [], []
    for b in range(levels):
        mix = lo_mix.at[:, b] if b < lo_levels else hi_mix.at[:, b - lo_levels]
        mix_copies.append(
            [
                pltpu.make_async_copy(
                    mix.at[pl.ds(side * half, half)], mix_v.at[b, side, held], mix_sem.at[b, side]
                )
                for side in range(2)
            ]
        )
    for side in range(2):
        out_copies.append(
            pltpu.make_async_copy(
                leaf_out.at[pl.ds(side * half, half)], out_v.at[side, held], out_sem.at[side]
            )
        )
    def begin(batches):
        for copies in batches:
            for copy in copies:
                copy.start()

    begin(in_copies + [loc_copies[:EARLY]])

    for c in range(CHUNKS):
        for copy in in_copies[c]:
            copy.wait()
        if c == LOCAT:
            begin([loc_copies[EARLY:]])
        for j in range(c * part, (c + 1) * part):
            lhs = jnp.concatenate([in_v[j], in_v[j + half]], axis=0)
            low, high = pl.ds(j * leaf, leaf), pl.ds((j + half) * leaf, leaf)
            rhs = jnp.concatenate([src_v[:, low], src_v[:, high]], axis=0)
            both = lax.dot_general(
                lhs, rhs, (((1,), (1,)), ((), ())), preferred_element_type=jnp.float32
            )
            tile = jnp.where(low_lanes((rank, 2 * vecs)), both[:rank], both[rank:])
            work[0][j] = tile.astype(jnp.bfloat16)

    for b in range(local_levels - 1):
        loc_copies[b].wait()
        stride = 1 << b
        now, later = work[b % 2], work[(b + 1) % 2]

        def pair(i, _):
            for u in range(UNROLL // 2):
                p = i * (UNROLL // 2) + u
                j = (p // stride) * (2 * stride) + p % stride
                k = j + stride
                first, second = now[j], now[k]
                later[j] = mixed(first, second, loc_v[b, j], loc_v[b, j + half])
                later[k] = mixed(second, first, loc_v[b, k], loc_v[b, k + half])
            return 0

        lax.fori_loop(0, half // UNROLL, pair, 0)
        if b == LATE:
            begin(mix_copies + [out_copies])
    last = local_levels - 1
    entered = work[last % 2]
    loc_copies[last].wait()
    pl.semaphore_wait(barrier, levels)

    starts = [0]
    for delay in DELAYS[:levels]:
        starts.append(starts[-1] + delay)
    starts.append(starts[-1] + 1)

    def message(stage, g):
        tiles = pl.ds((g + 1) * GROUP, GROUP)
        return pltpu.make_async_remote_copy(
            own[stage].at[tiles],
            recv[stage].at[tiles],
            send_sem.at[stage],
            recv_sem.at[stage, g],
            device_id=partners[stage],
            device_id_type=MESH,
        )

    def receive(stage, g):
        @pl.when((g >= 0) & (g < groups))
        def _():
            message(stage - 1, g).wait_recv()

        @pl.when(g == 0)
        def _():
            for copy in mix_copies[stage - 1]:
                copy.wait()

    def mix(stage, g, u):
        place = (jnp.minimum(jnp.maximum(g, -1), groups) + 1) * GROUP + u
        if stage > 0:
            known = jnp.minimum(place, half + u)
            own[stage][place] = mixed(
                own[stage - 1][place],
                recv[stage - 1][place],
                mix_v[stage - 1, 0, known],
                mix_v[stage - 1, 1, known],
            )
        else:
            j = jnp.minimum(jnp.maximum(g, 0), groups - 1) * GROUP + u
            tile = entered[j]
            turned = jnp.concatenate([tile[:, vecs:], tile[:, :vecs]], axis=1)
            own[0][place] = mixed(tile, turned, loc_v[last, j], loc_v[last, j + half])

    def interpolate(g, u):
        place = (jnp.maximum(g, -1) + 1) * GROUP + u
        j = jnp.maximum(g, 0) * GROUP + u
        flat = own[levels][place].T
        for side in range(2):
            columns = pl.ds(pl.multiple_of((j + side * half) * leaf, leaf), leaf)
            result = jnp.dot(
                flat[side * vecs : (side + 1) * vecs],
                out_v[side, place],
                preferred_element_type=jnp.float32,
            )
            targets[:, columns] = result.astype(jnp.bfloat16)

    def step(t, _):
        for block in BLOCKS:
            for stage in block:
                if 0 < stage <= levels:
                    receive(stage, t - starts[stage])
            if levels + 1 in block:

                @pl.when(t == starts[levels + 1])
                def _():
                    for copy in out_copies:
                        copy.wait()

            @pl.when((t >= starts[min(block)]) & (t < starts[max(block)] + groups))
            def _():
                for u in range(GROUP):
                    for stage in block:
                        if stage > levels:
                            interpolate(t - starts[stage], u)
                        else:
                            mix(stage, t - starts[stage], u)

            for stage in block:
                g = t - starts[stage]
                if stage < levels:

                    @pl.when((g >= 0) & (g < groups))
                    def _():
                        message(stage, g).start()

        return 0

    lax.fori_loop(0, groups + starts[levels + 1], step, 0)

    for stage in range(levels):
        pltpu.make_async_remote_copy(
            own[stage].at[held],
            recv[stage].at[held],
            send_sem.at[stage],
            recv_sem.at[stage, 0],
            device_id=partners[stage],
            device_id_type=MESH,
        ).wait_send()


def body(sources, leaf_in, local_mix, lo_mix, hi_mix, leaf_out):
    blocks, rank, _ = leaf_in.shape
    vecs = sources.shape[0]
    local_levels = local_mix.shape[1]
    lo_levels, hi_levels = lo_mix.shape[1], hi_mix.shape[1]
    levels = lo_levels + hi_levels
    half = blocks // 2
    factors = (blocks,) + local_mix.shape[2:]
    bf16, dma = jnp.bfloat16, pltpu.SemaphoreType.DMA
    spared = pltpu.VMEM((half + 2 * GROUP, rank, 2 * vecs), bf16)
    return pl.pallas_call(
        functools.partial(kernel, lo_levels, hi_levels),
        out_shape=jax.ShapeDtypeStruct(sources.shape, bf16),
        in_specs=[pl.BlockSpec(memory_space=pltpu.HBM)] * 6,
        out_specs=pl.BlockSpec(memory_space=pltpu.VMEM),
        scratch_shapes=[
            pltpu.VMEM(sources.shape, bf16),
            pltpu.VMEM(leaf_in.shape, bf16),
            pltpu.VMEM((local_levels,) + factors, bf16),
            pltpu.VMEM((levels, 2, half + GROUP) + factors[1:], bf16),
            pltpu.VMEM((2, half + GROUP) + leaf_out.shape[1:], bf16),
        ]
        + [pltpu.VMEM((half, rank, 2 * vecs), bf16)] * 2
        + [spared] * (2 * levels + 1)
        + [
            dma((CHUNKS, 4)),
            dma((local_levels,)),
            dma((levels, 2)),
            dma((2,)),
            dma((levels,)),
            dma((levels, half // GROUP)),
        ],
        compiler_params=pltpu.CompilerParams(
            collective_id=0, has_side_effects=True, vmem_limit_bytes=50 * 1024 * 1024
        ),
        name="butterfly",
    )(sources, leaf_in, local_mix, lo_mix, hi_mix, leaf_out)


def solution(mesh):
    return jax.shard_map(
        body,
        mesh=mesh,
        in_specs=(
            P(None, ("hi", "lo")),
            P(("hi", "lo"), None, None),
            P(("hi", "lo"), None, None, None),
            P(("hi", "lo"), None, None, None),
            P(("hi", "lo"), None, None, None),
            P(("hi", "lo"), None, None),
        ),
        out_specs=P(None, ("hi", "lo")),
        check_vma=False,
    )
```

```python
import functools

import jax
import jax.numpy as jnp
from jax import lax
from jax.experimental import pallas as pl
from jax.experimental.pallas import tpu as pltpu
from jax.sharding import PartitionSpec as P

MESH = pl.DeviceIdType.MESH
LATE = 1
GROUP = 1
DELAYS = (3, 5, 6, 5, 6, 5, 6)
CHUNKS = 4
BLOCKS = ((8, 7, 6, 5), (4, 3, 2, 1, 0))
UNROLL = 32


def low_lanes(shape):
    return lax.broadcasted_iota(jnp.int32, shape, len(shape) - 1) < shape[-1] // 2


def mixed(own, partner, f_low, f_high):
    zero = jnp.zeros_like(own)
    low = low_lanes(own.shape)
    rhs = jnp.concatenate(
        [
            jnp.where(low, own, zero),
            jnp.where(low, partner, zero),
            jnp.where(low, zero, own),
            jnp.where(low, zero, partner),
        ],
        axis=0,
    )
    lhs = jnp.concatenate([f_low, f_high], axis=1)
    return jnp.dot(lhs, rhs, preferred_element_type=jnp.float32).astype(jnp.bfloat16)


def kernel(lo_levels, hi_levels, *refs):
    levels = lo_levels + hi_levels
    sources, leaf_in, local_mix, lo_mix, hi_mix, leaf_out, targets = refs[:7]
    src_v, in_v, loc_v, mix_v, out_v = refs[7:12]
    work = refs[12:14]
    own = refs[14 : 15 + levels]
    recv = refs[15 + levels : 15 + 2 * levels]
    in_sem, loc_sem, mix_sem, out_sem, send_sem, recv_sem = refs[15 + 2 * levels :]
    blocks, rank, leaf = leaf_in.shape
    vecs = sources.shape[0]
    half = blocks // 2
    local_levels = local_mix.shape[1]
    groups = half // GROUP
    hi, lo = lax.axis_index("hi"), lax.axis_index("lo")

    def flipped(index, bit):
        stride = 1 << bit
        return index + stride - 2 * stride * ((index // stride) % 2)

    partners = [(hi, flipped(lo, b)) for b in range(lo_levels)]
    partners += [(flipped(hi, b), lo) for b in range(hi_levels)]

    barrier = pltpu.get_barrier_semaphore()
    for partner in partners:
        pl.semaphore_signal(barrier, inc=1, device_id=partner, device_id_type=MESH)

    part = half // CHUNKS
    in_copies = []
    for c in range(CHUNKS):
        copies = []
        for side in range(2):
            first = side * half + c * part
            columns = pl.ds(first * leaf, part * leaf)
            rows = pl.ds(first, part)
            copies.append(
                pltpu.make_async_copy(
                    sources.at[:, columns], src_v.at[:, columns], in_sem.at[c, 2 * side]
                )
            )
            copies.append(
                pltpu.make_async_copy(leaf_in.at[rows], in_v.at[rows], in_sem.at[c, 2 * side + 1])
            )
        in_copies.append(copies)
    loc_copies = [
        pltpu.make_async_copy(local_mix.at[:, b], loc_v.at[b], loc_sem.at[b])
        for b in range(local_levels)
    ]
    held = pl.ds(GROUP, half)
    mix_copies, out_copies = [], []
    for b in range(levels):
        mix = lo_mix.at[:, b] if b < lo_levels else hi_mix.at[:, b - lo_levels]
        mix_copies.append(
            [
                pltpu.make_async_copy(
                    mix.at[pl.ds(side * half, half)], mix_v.at[b, side, held], mix_sem.at[b, side]
                )
                for side in range(2)
            ]
        )
    for side in range(2):
        out_copies.append(
            pltpu.make_async_copy(
                leaf_out.at[pl.ds(side * half, half)], out_v.at[side, held], out_sem.at[side]
            )
        )
    for copies in in_copies:
        for copy in copies:
            copy.start(priority=0)
    for copy in loc_copies:
        copy.start(priority=1)

    for c in range(CHUNKS):
        for copy in in_copies[c]:
            copy.wait()
        for j in range(c * part, (c + 1) * part):
            lhs = jnp.concatenate([in_v[j], in_v[j + half]], axis=0)
            low, high = pl.ds(j * leaf, leaf), pl.ds((j + half) * leaf, leaf)
            rhs = jnp.concatenate([src_v[:, low], src_v[:, high]], axis=0)
            both = lax.dot_general(
                lhs, rhs, (((1,), (1,)), ((), ())), preferred_element_type=jnp.float32
            )
            tile = jnp.where(low_lanes((rank, 2 * vecs)), both[:rank], both[rank:])
            work[0][j] = tile.astype(jnp.bfloat16)

    for b in range(local_levels - 1):
        loc_copies[b].wait()
        if b == LATE:
            for copies in mix_copies + [out_copies]:
                for copy in copies:
                    copy.start(priority=1)
        stride = 1 << b
        now, later = work[b % 2], work[(b + 1) % 2]

        def pair(i, _):
            for u in range(UNROLL // 2):
                p = i * (UNROLL // 2) + u
                j = (p // stride) * (2 * stride) + p % stride
                k = j + stride
                first, second = now[j], now[k]
                later[j] = mixed(first, second, loc_v[b, j], loc_v[b, j + half])
                later[k] = mixed(second, first, loc_v[b, k], loc_v[b, k + half])
            return 0

        lax.fori_loop(0, half // UNROLL, pair, 0)
    last = local_levels - 1
    entered = work[last % 2]
    loc_copies[last].wait()
    pl.semaphore_wait(barrier, levels)

    starts = [0]
    for delay in DELAYS[:levels]:
        starts.append(starts[-1] + delay)
    starts.append(starts[-1] + 1)

    def message(stage, g):
        tiles = pl.ds((g + 1) * GROUP, GROUP)
        return pltpu.make_async_remote_copy(
            own[stage].at[tiles],
            recv[stage].at[tiles],
            send_sem.at[stage],
            recv_sem.at[stage, g],
            device_id=partners[stage],
            device_id_type=MESH,
        )

    def receive(stage, g):
        @pl.when((g >= 0) & (g < groups))
        def _():
            message(stage - 1, g).wait_recv()

        @pl.when(g == 0)
        def _():
            for copy in mix_copies[stage - 1]:
                copy.wait()

    def mix(stage, g, u):
        place = (jnp.minimum(jnp.maximum(g, -1), groups) + 1) * GROUP + u
        if stage > 0:
            known = jnp.minimum(place, half + u)
            own[stage][place] = mixed(
                own[stage - 1][place],
                recv[stage - 1][place],
                mix_v[stage - 1, 0, known],
                mix_v[stage - 1, 1, known],
            )
        else:
            j = jnp.minimum(jnp.maximum(g, 0), groups - 1) * GROUP + u
            tile = entered[j]
            turned = jnp.concatenate([tile[:, vecs:], tile[:, :vecs]], axis=1)
            own[0][place] = mixed(tile, turned, loc_v[last, j], loc_v[last, j + half])

    def interpolate(g, u):
        place = (jnp.maximum(g, -1) + 1) * GROUP + u
        j = jnp.maximum(g, 0) * GROUP + u
        flat = own[levels][place].T
        for side in range(2):
            columns = pl.ds(pl.multiple_of((j + side * half) * leaf, leaf), leaf)
            result = jnp.dot(
                flat[side * vecs : (side + 1) * vecs],
                out_v[side, place],
                preferred_element_type=jnp.float32,
            )
            targets[:, columns] = result.astype(jnp.bfloat16)

    def step(t, _):
        for block in BLOCKS:
            for stage in block:
                if 0 < stage <= levels:
                    receive(stage, t - starts[stage])
            if levels + 1 in block:

                @pl.when(t == starts[levels + 1])
                def _():
                    for copy in out_copies:
                        copy.wait()

            @pl.when((t >= starts[min(block)]) & (t < starts[max(block)] + groups))
            def _():
                for u in range(GROUP):
                    for stage in block:
                        if stage > levels:
                            interpolate(t - starts[stage], u)
                        else:
                            mix(stage, t - starts[stage], u)

            for stage in block:
                g = t - starts[stage]
                if stage < levels:

                    @pl.when((g >= 0) & (g < groups))
                    def _():
                        message(stage, g).start()

        return 0

    lax.fori_loop(0, groups + starts[levels + 1], step, 0)

    for stage in range(levels):
        pltpu.make_async_remote_copy(
            own[stage].at[held],
            recv[stage].at[held],
            send_sem.at[stage],
            recv_sem.at[stage, 0],
            device_id=partners[stage],
            device_id_type=MESH,
        ).wait_send()


def body(sources, leaf_in, local_mix, lo_mix, hi_mix, leaf_out):
    blocks, rank, _ = leaf_in.shape
    vecs = sources.shape[0]
    local_levels = local_mix.shape[1]
    lo_levels, hi_levels = lo_mix.shape[1], hi_mix.shape[1]
    levels = lo_levels + hi_levels
    half = blocks // 2
    factors = (blocks,) + local_mix.shape[2:]
    bf16, dma = jnp.bfloat16, pltpu.SemaphoreType.DMA
    spared = pltpu.VMEM((half + 2 * GROUP, rank, 2 * vecs), bf16)
    return pl.pallas_call(
        functools.partial(kernel, lo_levels, hi_levels),
        out_shape=jax.ShapeDtypeStruct(sources.shape, bf16),
        in_specs=[pl.BlockSpec(memory_space=pltpu.HBM)] * 6,
        out_specs=pl.BlockSpec(memory_space=pltpu.VMEM),
        scratch_shapes=[
            pltpu.VMEM(sources.shape, bf16),
            pltpu.VMEM(leaf_in.shape, bf16),
            pltpu.VMEM((local_levels,) + factors, bf16),
            pltpu.VMEM((levels, 2, half + GROUP) + factors[1:], bf16),
            pltpu.VMEM((2, half + GROUP) + leaf_out.shape[1:], bf16),
        ]
        + [pltpu.VMEM((half, rank, 2 * vecs), bf16)] * 2
        + [spared] * (2 * levels + 1)
        + [
            dma((CHUNKS, 4)),
            dma((local_levels,)),
            dma((levels, 2)),
            dma((2,)),
            dma((levels,)),
            dma((levels, half // GROUP)),
        ],
        compiler_params=pltpu.CompilerParams(
            collective_id=0, has_side_effects=True, vmem_limit_bytes=50 * 1024 * 1024
        ),
        name="butterfly",
    )(sources, leaf_in, local_mix, lo_mix, hi_mix, leaf_out)


def solution(mesh):
    return jax.shard_map(
        body,
        mesh=mesh,
        in_specs=(
            P(None, ("hi", "lo")),
            P(("hi", "lo"), None, None),
            P(("hi", "lo"), None, None, None),
            P(("hi", "lo"), None, None, None),
            P(("hi", "lo"), None, None, None),
            P(("hi", "lo"), None, None),
        ),
        out_specs=P(None, ("hi", "lo")),
        check_vma=False,
    )
```

```python
import functools

import jax
import jax.numpy as jnp
from jax import lax
from jax.experimental import pallas as pl
from jax.experimental.pallas import tpu as pltpu
from jax.sharding import PartitionSpec as P

MESH = pl.DeviceIdType.MESH
LATE = 1
TWO = 24
FARN = 8
DIRECT = 7
GROUP = 1
DELAYS = (3, 5, 6, 5, 6, 5, 6)
CHUNKS = 4
BLOCKS = ((10, 9), (8, 7, 6, 5), (4, 3, 2, 1, 0))
UNROLL = 32


def low_lanes(shape):
    return lax.broadcasted_iota(jnp.int32, shape, len(shape) - 1) < shape[-1] // 2


def mixed(own, partner, f_low, f_high):
    zero = jnp.zeros_like(own)
    low = low_lanes(own.shape)
    rhs = jnp.concatenate(
        [
            jnp.where(low, own, zero),
            jnp.where(low, partner, zero),
            jnp.where(low, zero, own),
            jnp.where(low, zero, partner),
        ],
        axis=0,
    )
    lhs = jnp.concatenate([f_low, f_high], axis=1)
    return jnp.dot(lhs, rhs, preferred_element_type=jnp.float32).astype(jnp.bfloat16)


def kernel(lo_levels, hi_levels, *refs):
    levels = lo_levels + hi_levels
    sources, leaf_in, local_mix, lo_mix, hi_mix, leaf_out, targets = refs[:7]
    src_v, in_v, loc_v, mix_v, out_v = refs[7:12]
    work = refs[12:14]
    own = refs[14 : 15 + levels]
    recv = refs[15 + levels : 16 + 2 * levels]
    far_v = refs[16 + 2 * levels]
    in_sem, loc_sem, mix_sem, out_sem, send_sem, recv_sem, far_send, far_recv = refs[17 + 2 * levels :]
    blocks, rank, leaf = leaf_in.shape
    vecs = sources.shape[0]
    half = blocks // 2
    local_levels = local_mix.shape[1]
    groups = half // GROUP
    far_tiles = (groups - TWO) * GROUP // (FARN // 2)
    hi, lo = lax.axis_index("hi"), lax.axis_index("lo")

    def flipped(index, bit):
        stride = 1 << bit
        return index + stride - 2 * stride * ((index // stride) % 2)

    partners = [(hi, flipped(lo, b)) for b in range(lo_levels)]
    partners += [(flipped(hi, b), lo) for b in range(hi_levels)]
    partners.append((flipped(flipped(hi, hi_levels - 2), hi_levels - 1), lo))

    barrier = pltpu.get_barrier_semaphore()
    for partner in partners:
        pl.semaphore_signal(barrier, inc=1, device_id=partner, device_id_type=MESH)

    part = half // CHUNKS
    in_copies = []
    for c in range(CHUNKS):
        copies = []
        for side in range(2):
            first = side * half + c * part
            columns = pl.ds(first * leaf, part * leaf)
            rows = pl.ds(first, part)
            copies.append(
                pltpu.make_async_copy(
                    sources.at[:, columns], src_v.at[:, columns], in_sem.at[c, 2 * side]
                )
            )
            copies.append(
                pltpu.make_async_copy(leaf_in.at[rows], in_v.at[rows], in_sem.at[c, 2 * side + 1])
            )
        in_copies.append(copies)
    loc_copies = [
        pltpu.make_async_copy(local_mix.at[:, b], loc_v.at[b], loc_sem.at[b])
        for b in range(local_levels)
    ]
    held = pl.ds(GROUP, half)
    mix_copies, out_copies = [], []
    for b in range(levels):
        mix = lo_mix.at[:, b] if b < lo_levels else hi_mix.at[:, b - lo_levels]
        mix_copies.append(
            [
                pltpu.make_async_copy(
                    mix.at[pl.ds(side * half, half)], mix_v.at[b, side, held], mix_sem.at[b, side]
                )
                for side in range(2)
            ]
        )
    for side in range(2):
        out_copies.append(
            pltpu.make_async_copy(
                leaf_out.at[pl.ds(side * half, half)], out_v.at[side, held], out_sem.at[side]
            )
        )
    for copies in in_copies:
        for copy in copies:
            copy.start(priority=0)
    for copy in loc_copies:
        copy.start(priority=1)

    def far(k):
        side, first = k % 2, TWO * GROUP + k // 2 * far_tiles
        return pltpu.make_async_remote_copy(
            hi_mix.at[pl.ds(side * half + first, far_tiles), hi_levels - 2],
            far_v.at[side, pl.ds(GROUP + first, far_tiles)],
            far_send.at[k],
            far_recv.at[k],
            device_id=partners[levels - 1],
            device_id_type=MESH,
        )

    for c in range(CHUNKS):
        for copy in in_copies[c]:
            copy.wait()
        if c == 0:
            pl.semaphore_wait(barrier, levels + 1)
            for k in range(FARN):
                far(k).start()
        for j in range(c * part, (c + 1) * part):
            lhs = jnp.concatenate([in_v[j], in_v[j + half]], axis=0)
            low, high = pl.ds(j * leaf, leaf), pl.ds((j + half) * leaf, leaf)
            rhs = jnp.concatenate([src_v[:, low], src_v[:, high]], axis=0)
            both = lax.dot_general(
                lhs, rhs, (((1,), (1,)), ((), ())), preferred_element_type=jnp.float32
            )
            tile = jnp.where(low_lanes((rank, 2 * vecs)), both[:rank], both[rank:])
            work[0][j] = tile.astype(jnp.bfloat16)

    for b in range(local_levels - 1):
        loc_copies[b].wait()
        if b == LATE:
            for copies in mix_copies + [out_copies]:
                for copy in copies:
                    copy.start(priority=1)
        stride = 1 << b
        now, later = work[b % 2], work[(b + 1) % 2]

        def pair(i, _):
            for u in range(UNROLL // 2):
                p = i * (UNROLL // 2) + u
                j = (p // stride) * (2 * stride) + p % stride
                k = j + stride
                first, second = now[j], now[k]
                later[j] = mixed(first, second, loc_v[b, j], loc_v[b, j + half])
                later[k] = mixed(second, first, loc_v[b, k], loc_v[b, k + half])
            return 0

        lax.fori_loop(0, half // UNROLL, pair, 0)
    last = local_levels - 1
    entered = work[last % 2]
    loc_copies[last].wait()

    near, both = levels - 2, levels + 2
    starts = [0]
    for delay in DELAYS:
        starts.append(starts[-1] + delay)
    starts.append(starts[-1] + 1)
    starts += [starts[near] + DIRECT, starts[near] + DIRECT + 1]
    spans = [(0, groups)] * (near + 1) + [(0, TWO)] * 3 + [(TWO, groups)] * 2

    def message(level, g, source):
        tiles = pl.ds((g + 1) * GROUP, GROUP)
        return pltpu.make_async_remote_copy(
            own[source].at[tiles],
            recv[level].at[tiles],
            send_sem.at[level],
            recv_sem.at[level, g],
            device_id=partners[level],
            device_id_type=MESH,
        )

    def receive(stage, g):
        first, end = spans[stage]
        wanted = (near, near + 1, near + 2) if stage == both else (stage - 1,)

        @pl.when((g >= first) & (g < end))
        def _():
            for level in wanted:
                message(level, g, 0).wait_recv()

        if stage == both:
            count = far_tiles // GROUP

            @pl.when((g >= first) & (g < end) & ((g - first) % count == 0))
            def _():
                for side in range(2):
                    k = (g - first) // count * 2 + side
                    rows = pl.ds((g + 1) * GROUP, far_tiles)
                    pltpu.make_async_remote_copy(
                        far_v.at[side, rows],
                        far_v.at[side, rows],
                        far_send.at[k],
                        far_recv.at[k],
                        device_id=partners[levels - 1],
                        device_id_type=MESH,
                    ).wait_recv()

        else:

            @pl.when(g == 0)
            def _():
                for copy in mix_copies[stage - 1]:
                    copy.wait()

    def located(stage, g, u):
        first, end = spans[stage]
        inside = jnp.clip(g - first + 1, 0, 1) * jnp.clip(end - g, 0, 1)
        return inside * (g + 1) * GROUP + u

    def factors(level, place):
        return mix_v[level, 0, place], mix_v[level, 1, place]

    def mix(stage, g, u):
        place = located(stage, g, u)
        if stage == both:
            a, b = near, near + 1
            here = mixed(own[a][place], recv[a][place], *factors(a, place))
            there = mixed(recv[b][place], recv[b + 1][place], far_v[0, place], far_v[1, place])
            own[levels][place] = mixed(here, there, *factors(b, place))
        elif stage > 0:
            own[stage][place] = mixed(
                own[stage - 1][place], recv[stage - 1][place], *factors(stage - 1, place)
            )
        else:
            j = jnp.clip(g, 0, groups - 1) * GROUP + u
            tile = entered[j]
            turned = jnp.concatenate([tile[:, vecs:], tile[:, :vecs]], axis=1)
            own[0][place] = mixed(tile, turned, loc_v[last, j], loc_v[last, j + half])

    def interpolate(stage, g, u):
        first, end = spans[stage]
        place = located(stage, g, u)
        j = jnp.clip(g, first, end - 1) * GROUP + u
        flat = own[levels][place].T
        for side in range(2):
            columns = pl.ds(pl.multiple_of((j + side * half) * leaf, leaf), leaf)
            result = jnp.dot(
                flat[side * vecs : (side + 1) * vecs],
                out_v[side, place],
                preferred_element_type=jnp.float32,
            )
            targets[:, columns] = result.astype(jnp.bfloat16)

    def step(t, _):
        for block in BLOCKS:
            for stage in block:
                if stage not in (0, levels + 1, levels + 3):
                    receive(stage, t - starts[stage])
            if levels + 1 in block:

                @pl.when(t == starts[levels + 1])
                def _():
                    for copy in out_copies:
                        copy.wait()

            enter = min(starts[s] + spans[s][0] for s in block)
            leave = max(starts[s] + spans[s][1] for s in block)

            @pl.when((t >= enter) & (t < leave))
            def _():
                for u in range(GROUP):
                    for stage in block:
                        if stage in (levels + 1, levels + 3):
                            interpolate(stage, t - starts[stage], u)
                        else:
                            mix(stage, t - starts[stage], u)

            for stage in block:
                g = t - starts[stage]
                first, end = spans[stage]
                if stage < levels:

                    @pl.when((g >= first) & (g < end))
                    def _():
                        message(stage, g, stage).start()

                if stage == near:

                    @pl.when((g >= TWO) & (g < groups))
                    def _():
                        message(near + 1, g, near).start()
                        message(near + 2, g, near).start()

        return 0

    steps = max(starts[s] + spans[s][1] for s in (levels + 1, levels + 3))
    lax.fori_loop(0, steps, step, 0)

    for k in range(FARN):
        far(k).wait_send()
    for level in range(levels + 1):
        first = TWO if level == levels else 0
        tiles = pl.ds((first + 1) * GROUP, (groups - first) * GROUP)
        pltpu.make_async_remote_copy(
            own[0].at[tiles],
            recv[level].at[tiles],
            send_sem.at[level],
            recv_sem.at[level, 0],
            device_id=partners[level],
            device_id_type=MESH,
        ).wait_send()


def body(sources, leaf_in, local_mix, lo_mix, hi_mix, leaf_out):
    blocks, rank, _ = leaf_in.shape
    vecs = sources.shape[0]
    local_levels = local_mix.shape[1]
    lo_levels, hi_levels = lo_mix.shape[1], hi_mix.shape[1]
    levels = lo_levels + hi_levels
    half = blocks // 2
    factors = (blocks,) + local_mix.shape[2:]
    bf16, dma = jnp.bfloat16, pltpu.SemaphoreType.DMA
    spared = pltpu.VMEM((half + 2 * GROUP, rank, 2 * vecs), bf16)
    return pl.pallas_call(
        functools.partial(kernel, lo_levels, hi_levels),
        out_shape=jax.ShapeDtypeStruct(sources.shape, bf16),
        in_specs=[pl.BlockSpec(memory_space=pltpu.HBM)] * 6,
        out_specs=pl.BlockSpec(memory_space=pltpu.VMEM),
        scratch_shapes=[
            pltpu.VMEM(sources.shape, bf16),
            pltpu.VMEM(leaf_in.shape, bf16),
            pltpu.VMEM((local_levels,) + factors, bf16),
            pltpu.VMEM((levels, 2, half + GROUP) + factors[1:], bf16),
            pltpu.VMEM((2, half + GROUP) + leaf_out.shape[1:], bf16),
        ]
        + [pltpu.VMEM((half, rank, 2 * vecs), bf16)] * 2
        + [spared] * (2 * levels + 2)
        + [pltpu.VMEM((2, half + GROUP) + factors[1:], bf16)]
        + [
            dma((CHUNKS, 4)),
            dma((local_levels,)),
            dma((levels, 2)),
            dma((2,)),
            dma((levels + 1,)),
            dma((levels + 1, half // GROUP)),
            dma((FARN,)),
            dma((FARN,)),
        ],
        compiler_params=pltpu.CompilerParams(
            collective_id=0, has_side_effects=True, vmem_limit_bytes=51 * 1024 * 1024
        ),
        name="butterfly",
    )(sources, leaf_in, local_mix, lo_mix, hi_mix, leaf_out)


def solution(mesh):
    return jax.shard_map(
        body,
        mesh=mesh,
        in_specs=(
            P(None, ("hi", "lo")),
            P(("hi", "lo"), None, None),
            P(("hi", "lo"), None, None, None),
            P(("hi", "lo"), None, None, None),
            P(("hi", "lo"), None, None, None),
            P(("hi", "lo"), None, None),
        ),
        out_specs=P(None, ("hi", "lo")),
        check_vma=False,
    )
```

```python
import functools

import jax
import jax.numpy as jnp
from jax import lax
from jax.experimental import pallas as pl
from jax.experimental.pallas import tpu as pltpu
from jax.sharding import PartitionSpec as P

MESH = pl.DeviceIdType.MESH
LATE = 1
TWO = 24
FARN = 8
DIRECT = 7
GROUP = 1
DELAYS = (4, 5, 6, 5, 6, 5, 6)
CHUNKS = 4
BLOCKS = ((10, 9), (8, 7, 6, 5), (4, 3, 2, 1, 0))
UNROLL = 32


def low_lanes(shape):
    return lax.broadcasted_iota(jnp.int32, shape, len(shape) - 1) < shape[-1] // 2


def mixed(own, partner, f_low, f_high):
    zero = jnp.zeros_like(own)
    low = low_lanes(own.shape)
    rhs = jnp.concatenate(
        [
            jnp.where(low, own, zero),
            jnp.where(low, partner, zero),
            jnp.where(low, zero, own),
            jnp.where(low, zero, partner),
        ],
        axis=0,
    )
    lhs = jnp.concatenate([f_low, f_high], axis=1)
    return jnp.dot(lhs, rhs, preferred_element_type=jnp.float32).astype(jnp.bfloat16)


def kernel(lo_levels, hi_levels, *refs):
    levels = lo_levels + hi_levels
    sources, leaf_in, local_mix, lo_mix, hi_mix, leaf_out, targets = refs[:7]
    src_v, in_v, loc_v, mix_v, out_v = refs[7:12]
    work = refs[12:14]
    own = refs[14 : 15 + levels]
    recv = refs[15 + levels : 16 + 2 * levels]
    far_v = refs[16 + 2 * levels]
    in_sem, loc_sem, mix_sem, out_sem, send_sem, recv_sem, far_send, far_recv = refs[17 + 2 * levels :]
    blocks, rank, leaf = leaf_in.shape
    vecs = sources.shape[0]
    half = blocks // 2
    local_levels = local_mix.shape[1]
    groups = half // GROUP
    far_tiles = (groups - TWO) * GROUP // (FARN // 2)
    hi, lo = lax.axis_index("hi"), lax.axis_index("lo")

    def flipped(index, bit):
        stride = 1 << bit
        return index + stride - 2 * stride * ((index // stride) % 2)

    partners = [(hi, flipped(lo, b)) for b in range(lo_levels)]
    partners += [(flipped(hi, b), lo) for b in range(hi_levels)]
    partners.append((flipped(flipped(hi, hi_levels - 2), hi_levels - 1), lo))

    barrier = pltpu.get_barrier_semaphore()
    for partner in partners:
        pl.semaphore_signal(barrier, inc=1, device_id=partner, device_id_type=MESH)

    part = half // CHUNKS
    in_copies = []
    for c in range(CHUNKS):
        copies = []
        for side in range(2):
            first = side * half + c * part
            columns = pl.ds(first * leaf, part * leaf)
            rows = pl.ds(first, part)
            copies.append(
                pltpu.make_async_copy(
                    sources.at[:, columns], src_v.at[:, columns], in_sem.at[c, 2 * side]
                )
            )
            copies.append(
                pltpu.make_async_copy(leaf_in.at[rows], in_v.at[rows], in_sem.at[c, 2 * side + 1])
            )
        in_copies.append(copies)
    loc_copies = [
        pltpu.make_async_copy(local_mix.at[:, b], loc_v.at[b], loc_sem.at[b])
        for b in range(local_levels)
    ]
    held = pl.ds(GROUP, half)
    mix_copies, out_copies = [], []
    for b in range(levels):
        mix = lo_mix.at[:, b] if b < lo_levels else hi_mix.at[:, b - lo_levels]
        mix_copies.append(
            [
                pltpu.make_async_copy(
                    mix.at[pl.ds(side * half, half)], mix_v.at[b, side, held], mix_sem.at[b, side]
                )
                for side in range(2)
            ]
        )
    for side in range(2):
        out_copies.append(
            pltpu.make_async_copy(
                leaf_out.at[pl.ds(side * half, half)], out_v.at[side, held], out_sem.at[side]
            )
        )
    for copies in in_copies:
        for copy in copies:
            copy.start(priority=0)
    for copy in loc_copies:
        copy.start(priority=1)

    def far(k):
        side, first = k % 2, TWO * GROUP + k // 2 * far_tiles
        return pltpu.make_async_remote_copy(
            hi_mix.at[pl.ds(side * half + first, far_tiles), hi_levels - 2],
            far_v.at[side, pl.ds(GROUP + first, far_tiles)],
            far_send.at[k],
            far_recv.at[k],
            device_id=partners[levels - 1],
            device_id_type=MESH,
        )

    for c in range(CHUNKS):
        for copy in in_copies[c]:
            copy.wait()
        if c == 0:
            pl.semaphore_wait(barrier, levels + 1)
            for k in range(FARN):
                far(k).start()
        for j in range(c * part, (c + 1) * part):
            lhs = jnp.concatenate([in_v[j], in_v[j + half]], axis=0)
            low, high = pl.ds(j * leaf, leaf), pl.ds((j + half) * leaf, leaf)
            rhs = jnp.concatenate([src_v[:, low], src_v[:, high]], axis=0)
            both = lax.dot_general(
                lhs, rhs, (((1,), (1,)), ((), ())), preferred_element_type=jnp.float32
            )
            tile = jnp.where(low_lanes((rank, 2 * vecs)), both[:rank], both[rank:])
            work[0][j] = tile.astype(jnp.bfloat16)

    for b in range(local_levels - 1):
        loc_copies[b].wait()
        if b == LATE:
            for copies in mix_copies + [out_copies]:
                for copy in copies:
                    copy.start(priority=1)
        stride = 1 << b
        now, later = work[b % 2], work[(b + 1) % 2]

        def pair(i, _):
            for u in range(UNROLL // 2):
                p = i * (UNROLL // 2) + u
                j = (p // stride) * (2 * stride) + p % stride
                k = j + stride
                first, second = now[j], now[k]
                later[j] = mixed(first, second, loc_v[b, j], loc_v[b, j + half])
                later[k] = mixed(second, first, loc_v[b, k], loc_v[b, k + half])
            return 0

        lax.fori_loop(0, half // UNROLL, pair, 0)
    last = local_levels - 1
    entered = work[last % 2]
    loc_copies[last].wait()

    near, both = levels - 2, levels + 2
    starts = [0]
    for delay in DELAYS:
        starts.append(starts[-1] + delay)
    starts.append(starts[-1] + 1)
    starts += [starts[near] + DIRECT, starts[near] + DIRECT + 1]
    spans = [(0, groups)] * (near + 1) + [(0, TWO)] * 3 + [(TWO, groups)] * 2

    def message(level, g, source):
        tiles = pl.ds((g + 1) * GROUP, GROUP)
        return pltpu.make_async_remote_copy(
            own[source].at[tiles],
            recv[level].at[tiles],
            send_sem.at[level],
            recv_sem.at[level, g],
            device_id=partners[level],
            device_id_type=MESH,
        )

    def receive(stage, g):
        first, end = spans[stage]
        wanted = (near, near + 1, near + 2) if stage == both else (stage - 1,)

        @pl.when((g >= first) & (g < end))
        def _():
            for level in wanted:
                message(level, g, 0).wait_recv()

        if stage == both:
            count = far_tiles // GROUP

            @pl.when((g >= first) & (g < end) & ((g - first) % count == 0))
            def _():
                for side in range(2):
                    k = (g - first) // count * 2 + side
                    rows = pl.ds((g + 1) * GROUP, far_tiles)
                    pltpu.make_async_remote_copy(
                        far_v.at[side, rows],
                        far_v.at[side, rows],
                        far_send.at[k],
                        far_recv.at[k],
                        device_id=partners[levels - 1],
                        device_id_type=MESH,
                    ).wait_recv()

        else:

            @pl.when(g == 0)
            def _():
                for copy in mix_copies[stage - 1]:
                    copy.wait()

    def located(stage, g, u):
        first, end = spans[stage]
        inside = jnp.clip(g - first + 1, 0, 1) * jnp.clip(end - g, 0, 1)
        return inside * (g + 1) * GROUP + u

    def factors(level, place):
        return mix_v[level, 0, place], mix_v[level, 1, place]

    def mix(stage, g, u):
        place = located(stage, g, u)
        if stage == both:
            a, b = near, near + 1
            here = mixed(own[a][place], recv[a][place], *factors(a, place))
            there = mixed(recv[b][place], recv[b + 1][place], far_v[0, place], far_v[1, place])
            own[levels][place] = mixed(here, there, *factors(b, place))
        elif stage > 0:
            own[stage][place] = mixed(
                own[stage - 1][place], recv[stage - 1][place], *factors(stage - 1, place)
            )
        else:
            j = jnp.clip(g, 0, groups - 1) * GROUP + u
            tile = entered[j]
            turned = jnp.concatenate([tile[:, vecs:], tile[:, :vecs]], axis=1)
            own[0][place] = mixed(tile, turned, loc_v[last, j], loc_v[last, j + half])

    def interpolate(stage, g, u):
        first, end = spans[stage]
        place = located(stage, g, u)
        j = jnp.clip(g, first, end - 1) * GROUP + u
        flat = own[levels][place].T
        for side in range(2):
            columns = pl.ds(pl.multiple_of((j + side * half) * leaf, leaf), leaf)
            result = jnp.dot(
                flat[side * vecs : (side + 1) * vecs],
                out_v[side, place],
                preferred_element_type=jnp.float32,
            )
            targets[:, columns] = result.astype(jnp.bfloat16)

    def step(t, _):
        for block in BLOCKS:
            for stage in block:
                if stage not in (0, levels + 1, levels + 3):
                    receive(stage, t - starts[stage])
            if levels + 1 in block:

                @pl.when(t == starts[levels + 1])
                def _():
                    for copy in out_copies:
                        copy.wait()

            enter = min(starts[s] + spans[s][0] for s in block)
            leave = max(starts[s] + spans[s][1] for s in block)

            @pl.when((t >= enter) & (t < leave))
            def _():
                for u in range(GROUP):
                    for stage in block:
                        if stage in (levels + 1, levels + 3):
                            interpolate(stage, t - starts[stage], u)
                        else:
                            mix(stage, t - starts[stage], u)

            for stage in block:
                g = t - starts[stage]
                first, end = spans[stage]
                if stage < levels:

                    @pl.when((g >= first) & (g < end))
                    def _():
                        message(stage, g, stage).start()

                if stage == near:

                    @pl.when((g >= TWO) & (g < groups))
                    def _():
                        message(near + 1, g, near).start()
                        message(near + 2, g, near).start()

        return 0

    steps = max(starts[s] + spans[s][1] for s in (levels + 1, levels + 3))
    lax.fori_loop(0, steps, step, 0)

    for k in range(FARN):
        far(k).wait_send()
    for level in range(levels + 1):
        first = TWO if level == levels else 0
        tiles = pl.ds((first + 1) * GROUP, (groups - first) * GROUP)
        pltpu.make_async_remote_copy(
            own[0].at[tiles],
            recv[level].at[tiles],
            send_sem.at[level],
            recv_sem.at[level, 0],
            device_id=partners[level],
            device_id_type=MESH,
        ).wait_send()


def body(sources, leaf_in, local_mix, lo_mix, hi_mix, leaf_out):
    blocks, rank, _ = leaf_in.shape
    vecs = sources.shape[0]
    local_levels = local_mix.shape[1]
    lo_levels, hi_levels = lo_mix.shape[1], hi_mix.shape[1]
    levels = lo_levels + hi_levels
    half = blocks // 2
    factors = (blocks,) + local_mix.shape[2:]
    bf16, dma = jnp.bfloat16, pltpu.SemaphoreType.DMA
    spared = pltpu.VMEM((half + 2 * GROUP, rank, 2 * vecs), bf16)
    return pl.pallas_call(
        functools.partial(kernel, lo_levels, hi_levels),
        out_shape=jax.ShapeDtypeStruct(sources.shape, bf16),
        in_specs=[pl.BlockSpec(memory_space=pltpu.HBM)] * 6,
        out_specs=pl.BlockSpec(memory_space=pltpu.VMEM),
        scratch_shapes=[
            pltpu.VMEM(sources.shape, bf16),
            pltpu.VMEM(leaf_in.shape, bf16),
            pltpu.VMEM((local_levels,) + factors, bf16),
            pltpu.VMEM((levels, 2, half + GROUP) + factors[1:], bf16),
            pltpu.VMEM((2, half + GROUP) + leaf_out.shape[1:], bf16),
        ]
        + [pltpu.VMEM((half, rank, 2 * vecs), bf16)] * 2
        + [spared] * (2 * levels + 2)
        + [pltpu.VMEM((2, half + GROUP) + factors[1:], bf16)]
        + [
            dma((CHUNKS, 4)),
            dma((local_levels,)),
            dma((levels, 2)),
            dma((2,)),
            dma((levels + 1,)),
            dma((levels + 1, half // GROUP)),
            dma((FARN,)),
            dma((FARN,)),
        ],
        compiler_params=pltpu.CompilerParams(
            collective_id=0, has_side_effects=True, vmem_limit_bytes=51 * 1024 * 1024
        ),
        name="butterfly",
    )(sources, leaf_in, local_mix, lo_mix, hi_mix, leaf_out)


def solution(mesh):
    return jax.shard_map(
        body,
        mesh=mesh,
        in_specs=(
            P(None, ("hi", "lo")),
            P(("hi", "lo"), None, None),
            P(("hi", "lo"), None, None, None),
            P(("hi", "lo"), None, None, None),
            P(("hi", "lo"), None, None, None),
            P(("hi", "lo"), None, None),
        ),
        out_specs=P(None, ("hi", "lo")),
        check_vma=False,
    )
```

```python
import functools

import jax
import jax.numpy as jnp
from jax import lax
from jax.experimental import pallas as pl
from jax.experimental.pallas import tpu as pltpu
from jax.sharding import PartitionSpec as P

MESH = pl.DeviceIdType.MESH
LATE = 1
TWO = 24
FARN = 8
DIRECT = 7
GROUP = 1
DELAYS = (5, 5, 6, 5, 6, 5, 6)
CHUNKS = 4
BLOCKS = ((10, 9), (8, 7, 6, 5), (4, 3, 2, 1, 0))
UNROLL = 32


def low_lanes(shape):
    return lax.broadcasted_iota(jnp.int32, shape, len(shape) - 1) < shape[-1] // 2


def mixed(own, partner, f_low, f_high):
    zero = jnp.zeros_like(own)
    low = low_lanes(own.shape)
    rhs = jnp.concatenate(
        [
            jnp.where(low, own, zero),
            jnp.where(low, partner, zero),
            jnp.where(low, zero, own),
            jnp.where(low, zero, partner),
        ],
        axis=0,
    )
    lhs = jnp.concatenate([f_low, f_high], axis=1)
    return jnp.dot(lhs, rhs, preferred_element_type=jnp.float32).astype(jnp.bfloat16)


def kernel(lo_levels, hi_levels, *refs):
    levels = lo_levels + hi_levels
    sources, leaf_in, local_mix, lo_mix, hi_mix, leaf_out, targets = refs[:7]
    src_v, in_v, loc_v, mix_v, out_v = refs[7:12]
    work = refs[12:14]
    own = refs[14 : 15 + levels]
    recv = refs[15 + levels : 16 + 2 * levels]
    far_v = refs[16 + 2 * levels]
    in_sem, loc_sem, mix_sem, out_sem, send_sem, recv_sem, far_send, far_recv = refs[17 + 2 * levels :]
    blocks, rank, leaf = leaf_in.shape
    vecs = sources.shape[0]
    half = blocks // 2
    local_levels = local_mix.shape[1]
    groups = half // GROUP
    far_tiles = (groups - TWO) * GROUP // (FARN // 2)
    hi, lo = lax.axis_index("hi"), lax.axis_index("lo")

    def flipped(index, bit):
        stride = 1 << bit
        return index + stride - 2 * stride * ((index // stride) % 2)

    partners = [(hi, flipped(lo, b)) for b in range(lo_levels)]
    partners += [(flipped(hi, b), lo) for b in range(hi_levels)]
    partners.append((flipped(flipped(hi, hi_levels - 2), hi_levels - 1), lo))

    barrier = pltpu.get_barrier_semaphore()
    for partner in partners:
        pl.semaphore_signal(barrier, inc=1, device_id=partner, device_id_type=MESH)

    part = half // CHUNKS
    in_copies = []
    for c in range(CHUNKS):
        copies = []
        for side in range(2):
            first = side * half + c * part
            columns = pl.ds(first * leaf, part * leaf)
            rows = pl.ds(first, part)
            copies.append(
                pltpu.make_async_copy(
                    sources.at[:, columns], src_v.at[:, columns], in_sem.at[c, 2 * side]
                )
            )
            copies.append(
                pltpu.make_async_copy(leaf_in.at[rows], in_v.at[rows], in_sem.at[c, 2 * side + 1])
            )
        in_copies.append(copies)
    loc_copies = [
        pltpu.make_async_copy(local_mix.at[:, b], loc_v.at[b], loc_sem.at[b])
        for b in range(local_levels)
    ]
    held = pl.ds(GROUP, half)
    mix_copies, out_copies = [], []
    for b in range(levels):
        mix = lo_mix.at[:, b] if b < lo_levels else hi_mix.at[:, b - lo_levels]
        mix_copies.append(
            [
                pltpu.make_async_copy(
                    mix.at[pl.ds(side * half, half)], mix_v.at[b, side, held], mix_sem.at[b, side]
                )
                for side in range(2)
            ]
        )
    for side in range(2):
        out_copies.append(
            pltpu.make_async_copy(
                leaf_out.at[pl.ds(side * half, half)], out_v.at[side, held], out_sem.at[side]
            )
        )
    for copies in in_copies:
        for copy in copies:
            copy.start(priority=0)
    for copy in loc_copies:
        copy.start(priority=1)

    def far(k):
        side, first = k % 2, TWO * GROUP + k // 2 * far_tiles
        return pltpu.make_async_remote_copy(
            hi_mix.at[pl.ds(side * half + first, far_tiles), hi_levels - 2],
            far_v.at[side, pl.ds(GROUP + first, far_tiles)],
            far_send.at[k],
            far_recv.at[k],
            device_id=partners[levels - 1],
            device_id_type=MESH,
        )

    for c in range(CHUNKS):
        for copy in in_copies[c]:
            copy.wait()
        if c == 0:
            pl.semaphore_wait(barrier, levels + 1)
            for k in range(FARN):
                far(k).start()
        for j in range(c * part, (c + 1) * part):
            lhs = jnp.concatenate([in_v[j], in_v[j + half]], axis=0)
            low, high = pl.ds(j * leaf, leaf), pl.ds((j + half) * leaf, leaf)
            rhs = jnp.concatenate([src_v[:, low], src_v[:, high]], axis=0)
            both = lax.dot_general(
                lhs, rhs, (((1,), (1,)), ((), ())), preferred_element_type=jnp.float32
            )
            tile = jnp.where(low_lanes((rank, 2 * vecs)), both[:rank], both[rank:])
            work[0][j] = tile.astype(jnp.bfloat16)

    for b in range(local_levels - 1):
        loc_copies[b].wait()
        if b == LATE:
            for copies in mix_copies + [out_copies]:
                for copy in copies:
                    copy.start(priority=1)
        stride = 1 << b
        now, later = work[b % 2], work[(b + 1) % 2]

        def pair(i, _):
            for u in range(UNROLL // 2):
                p = i * (UNROLL // 2) + u
                j = (p // stride) * (2 * stride) + p % stride
                k = j + stride
                first, second = now[j], now[k]
                later[j] = mixed(first, second, loc_v[b, j], loc_v[b, j + half])
                later[k] = mixed(second, first, loc_v[b, k], loc_v[b, k + half])
            return 0

        lax.fori_loop(0, half // UNROLL, pair, 0)
    last = local_levels - 1
    entered = work[last % 2]
    loc_copies[last].wait()

    near, both = levels - 2, levels + 2
    starts = [0]
    for delay in DELAYS:
        starts.append(starts[-1] + delay)
    starts.append(starts[-1] + 1)
    starts += [starts[near] + DIRECT, starts[near] + DIRECT + 1]
    spans = [(0, groups)] * (near + 1) + [(0, TWO)] * 3 + [(TWO, groups)] * 2

    def message(level, g, source):
        tiles = pl.ds((g + 1) * GROUP, GROUP)
        return pltpu.make_async_remote_copy(
            own[source].at[tiles],
            recv[level].at[tiles],
            send_sem.at[level],
            recv_sem.at[level, g],
            device_id=partners[level],
            device_id_type=MESH,
        )

    def receive(stage, g):
        first, end = spans[stage]
        wanted = (near, near + 1, near + 2) if stage == both else (stage - 1,)

        @pl.when((g >= first) & (g < end))
        def _():
            for level in wanted:
                message(level, g, 0).wait_recv()

        if stage == both:
            count = far_tiles // GROUP

            @pl.when((g >= first) & (g < end) & ((g - first) % count == 0))
            def _():
                for side in range(2):
                    k = (g - first) // count * 2 + side
                    rows = pl.ds((g + 1) * GROUP, far_tiles)
                    pltpu.make_async_remote_copy(
                        far_v.at[side, rows],
                        far_v.at[side, rows],
                        far_send.at[k],
                        far_recv.at[k],
                        device_id=partners[levels - 1],
                        device_id_type=MESH,
                    ).wait_recv()

        else:

            @pl.when(g == 0)
            def _():
                for copy in mix_copies[stage - 1]:
                    copy.wait()

    def located(stage, g, u):
        first, end = spans[stage]
        inside = jnp.clip(g - first + 1, 0, 1) * jnp.clip(end - g, 0, 1)
        return inside * (g + 1) * GROUP + u

    def factors(level, place):
        return mix_v[level, 0, place], mix_v[level, 1, place]

    def mix(stage, g, u):
        place = located(stage, g, u)
        if stage == both:
            a, b = near, near + 1
            here = mixed(own[a][place], recv[a][place], *factors(a, place))
            there = mixed(recv[b][place], recv[b + 1][place], far_v[0, place], far_v[1, place])
            own[levels][place] = mixed(here, there, *factors(b, place))
        elif stage > 0:
            own[stage][place] = mixed(
                own[stage - 1][place], recv[stage - 1][place], *factors(stage - 1, place)
            )
        else:
            j = jnp.clip(g, 0, groups - 1) * GROUP + u
            tile = entered[j]
            turned = jnp.concatenate([tile[:, vecs:], tile[:, :vecs]], axis=1)
            own[0][place] = mixed(tile, turned, loc_v[last, j], loc_v[last, j + half])

    def interpolate(stage, g, u):
        first, end = spans[stage]
        place = located(stage, g, u)
        j = jnp.clip(g, first, end - 1) * GROUP + u
        flat = own[levels][place].T
        for side in range(2):
            columns = pl.ds(pl.multiple_of((j + side * half) * leaf, leaf), leaf)
            result = jnp.dot(
                flat[side * vecs : (side + 1) * vecs],
                out_v[side, place],
                preferred_element_type=jnp.float32,
            )
            targets[:, columns] = result.astype(jnp.bfloat16)

    def step(t, _):
        for block in BLOCKS:
            for stage in block:
                if stage not in (0, levels + 1, levels + 3):
                    receive(stage, t - starts[stage])
            if levels + 1 in block:

                @pl.when(t == starts[levels + 1])
                def _():
                    for copy in out_copies:
                        copy.wait()

            enter = min(starts[s] + spans[s][0] for s in block)
            leave = max(starts[s] + spans[s][1] for s in block)

            @pl.when((t >= enter) & (t < leave))
            def _():
                for u in range(GROUP):
                    for stage in block:
                        if stage in (levels + 1, levels + 3):
                            interpolate(stage, t - starts[stage], u)
                        else:
                            mix(stage, t - starts[stage], u)

            for stage in block:
                g = t - starts[stage]
                first, end = spans[stage]
                if stage < levels:

                    @pl.when((g >= first) & (g < end))
                    def _():
                        message(stage, g, stage).start()

                if stage == near:

                    @pl.when((g >= TWO) & (g < groups))
                    def _():
                        message(near + 1, g, near).start()
                        message(near + 2, g, near).start()

        return 0

    steps = max(starts[s] + spans[s][1] for s in (levels + 1, levels + 3))
    lax.fori_loop(0, steps, step, 0)

    for k in range(FARN):
        far(k).wait_send()
    for level in range(levels + 1):
        first = TWO if level == levels else 0
        tiles = pl.ds((first + 1) * GROUP, (groups - first) * GROUP)
        pltpu.make_async_remote_copy(
            own[0].at[tiles],
            recv[level].at[tiles],
            send_sem.at[level],
            recv_sem.at[level, 0],
            device_id=partners[level],
            device_id_type=MESH,
        ).wait_send()


def body(sources, leaf_in, local_mix, lo_mix, hi_mix, leaf_out):
    blocks, rank, _ = leaf_in.shape
    vecs = sources.shape[0]
    local_levels = local_mix.shape[1]
    lo_levels, hi_levels = lo_mix.shape[1], hi_mix.shape[1]
    levels = lo_levels + hi_levels
    half = blocks // 2
    factors = (blocks,) + local_mix.shape[2:]
    bf16, dma = jnp.bfloat16, pltpu.SemaphoreType.DMA
    spared = pltpu.VMEM((half + 2 * GROUP, rank, 2 * vecs), bf16)
    return pl.pallas_call(
        functools.partial(kernel, lo_levels, hi_levels),
        out_shape=jax.ShapeDtypeStruct(sources.shape, bf16),
        in_specs=[pl.BlockSpec(memory_space=pltpu.HBM)] * 6,
        out_specs=pl.BlockSpec(memory_space=pltpu.VMEM),
        scratch_shapes=[
            pltpu.VMEM(sources.shape, bf16),
            pltpu.VMEM(leaf_in.shape, bf16),
            pltpu.VMEM((local_levels,) + factors, bf16),
            pltpu.VMEM((levels, 2, half + GROUP) + factors[1:], bf16),
            pltpu.VMEM((2, half + GROUP) + leaf_out.shape[1:], bf16),
        ]
        + [pltpu.VMEM((half, rank, 2 * vecs), bf16)] * 2
        + [spared] * (2 * levels + 2)
        + [pltpu.VMEM((2, half + GROUP) + factors[1:], bf16)]
        + [
            dma((CHUNKS, 4)),
            dma((local_levels,)),
            dma((levels, 2)),
            dma((2,)),
            dma((levels + 1,)),
            dma((levels + 1, half // GROUP)),
            dma((FARN,)),
            dma((FARN,)),
        ],
        compiler_params=pltpu.CompilerParams(
            collective_id=0, has_side_effects=True, vmem_limit_bytes=51 * 1024 * 1024
        ),
        name="butterfly",
    )(sources, leaf_in, local_mix, lo_mix, hi_mix, leaf_out)


def solution(mesh):
    return jax.shard_map(
        body,
        mesh=mesh,
        in_specs=(
            P(None, ("hi", "lo")),
            P(("hi", "lo"), None, None),
            P(("hi", "lo"), None, None, None),
            P(("hi", "lo"), None, None, None),
            P(("hi", "lo"), None, None, None),
            P(("hi", "lo"), None, None),
        ),
        out_specs=P(None, ("hi", "lo")),
        check_vma=False,
    )
```
